256 devices in a mesh: dp: 128 (over x, z_lo, y, core), mp: 2 (over z_hi).
Axes of the slice: x: 4, y: 4, z: 8 (z_hi: 2, z_lo: 4; z = z_hi * 4 + z_lo), core: 2. Of those that a mesh axis runs over, the one named last changes fastest.
Arguments:
- hidden_in: bfloat16 [16384, 2048], P('dp'), may hold values from -6 to 6
- depth: int32 [16384], P('dp'), may hold values from 1 to 3
- destination: int32 [3, 16384], P(None, 'dp'), may hold values from 0 to 16383, as said below
- weight: bfloat16 [2048, 2048], P('dp', 'mp'), may hold values from -0.125 to 0.125
- cotangent: bfloat16 [16384, 2048], P('dp'), may hold values from -24 to 24
Outputs:
- final: bfloat16 [16384, 2048], P('dp')
- grad_in: bfloat16 [16384, 2048], P('dp')
- grad_weight: float32 [2048, 2048], P('dp', 'mp')
The draws below stay inside these ranges and needn't reach their ends.
Inputs may be any that keep to these rules, and one draw needn't show every extreme that they name: For each recursion, destination is a permutation of the 16384 rows; position p lies on device p // 128. The rows of one device go to 64 devices, exactly 2 rows to each.
All inputs are finite; a program needn't handle non-finite values.
Results may differ from the reference program's by a relative error of at most 0.017.
Values may be sent and summed in bfloat16 or wider, within the bound.
No kernel may reach another device: no remote copies, remote signals or barrier semaphores. Data moves between devices by JAX's collectives and lax.ppermute only.
A program may use at most 128 MiB of HBM per device.

```python
import jax
import jax.numpy as jnp
from jax import lax

D = 2048
INNER = 2048
R_DEV = 128
NR = 16384
N_DP = 128
N_MP = 2


def draw_destination(key, part):
    key = jax.random.fold_in(key, 11)
    cap = max(2, 2 * R_DEV // N_DP)
    groups = R_DEV // cap
    tables = []
    for step in range(3):
        first, second, third = jax.random.split(jax.random.fold_in(key, step), 3)
        scores = jax.random.permutation(first, N_DP).astype(jnp.int32)
        scores = scores.at[N_DP - 1].set(-3).at[1].set(-2).at[N_DP // 2].set(-1)
        offsets = jnp.argsort(scores, stable=True).astype(jnp.int32)[:groups]
        base = jnp.tile(jnp.arange(R_DEV, dtype=jnp.int32)[None, :], (N_DP, 1))
        order = jax.random.permutation(second, base, axis=1, independent=True)
        slots = jax.random.permutation(third, base, axis=1, independent=True)
        position = jnp.arange(R_DEV, dtype=jnp.int32)
        group_of = position // cap
        source = jnp.arange(N_DP, dtype=jnp.int32)[:, None]
        target_dev = (source + offsets[group_of][None, :]) % N_DP
        within = jnp.broadcast_to(position[None, :], (N_DP, R_DEV))
        slot = slots[target_dev, within]
        value = target_dev * R_DEV + slot
        table = jnp.zeros((N_DP, R_DEV), jnp.int32).at[jnp.broadcast_to(source, (N_DP, R_DEV)), order].set(value)
        tables.append(table.reshape(-1))
    return jnp.stack(tables).astype(jnp.int32)


def touch_ends(array, key, low, top_value):
    shape = array.shape
    place = [jax.random.randint(jax.random.fold_in(key, axis), (), 0, shape[axis]) for axis in range(len(shape))]
    array = array.at[tuple(place)].set(low)
    longest = shape.index(max(shape))
    place[longest] = (place[longest] + 1) % shape[longest]
    return array.at[tuple(place)].set(top_value)


def raised(array, stream_key, source, target, shards_of, factor):
    owner, partner = [(jnp.arange(array.shape[axis_at]) // (array.shape[axis_at] // shards_of)).reshape([-1 if axis == axis_at else 1 for axis in range(array.ndim)]) for axis_at in (source, target)]
    chosen = jax.random.permutation(stream_key, shards_of)[partner]
    strong = (owner == chosen) | (owner == (partner + shards_of // 2) % shards_of)
    return jnp.where(strong, factor * array, array)


def block_levels(key, shape, cuts, low, top_value):
    level, own = 1.0, jax.random.fold_in(key, 6)
    for dim, parts in cuts:
        heights = jnp.exp(jax.random.uniform(jax.random.fold_in(own, dim), (parts,), jnp.float32, low / len(cuts), top_value / len(cuts)))
        level = level * jnp.repeat(heights, shape[dim] // parts).reshape([-1 if axis == dim else 1 for axis in range(len(shape))])
    return level


def scatter_about(key, dims, spread, reach, cuts=(), kind=jnp.bfloat16):
    result = jax.random.normal(key, dims, jnp.float32) * spread
    if len(cuts) > 0:
        result = block_levels(key, dims, cuts, -0.22, 0.18) * result
    return jnp.clip(result, min=-reach, max=reach).astype(kind)


def bell_draw_with(key, shape, deviation, most, shards, heavy, kind=jnp.bfloat16):
    drawn = deviation * jax.random.normal(key, shape, jnp.float32)
    if shards:
        drawn = drawn * block_levels(key, shape, shards, -0.22, 0.18)
    return jnp.clip(raised(drawn, jax.random.fold_in(key, 3), *heavy), -most, most).astype(kind)


def setup_inputs(seed: int = 0) -> dict:
    seeds = jax.random.split(jax.random.key(seed), 6)
    return {
        "hidden_in": scatter_about(seeds[0], (NR, D), 1.0, 6.0, ((0, 128),)),
        "depth": touch_ends(jax.random.randint(seeds[1], (NR,), 1, 4), jax.random.fold_in(seeds[1], 1), 1, 3).astype(jnp.int32),
        "destination": draw_destination(jax.random.fold_in(seeds[5], 71), 0),
        "weight": scatter_about(seeds[3], (D, INNER), D ** -0.5, 0.125, ((0, 128), (1, 2))),
        "cotangent": bell_draw_with(seeds[4], (NR, D), 1.0, 24.0, ((0, 128),), (0, 1, 128, 5.5)),
    }


def halves_product(left, weight):
    half = INNER // N_MP
    total = jnp.zeros((left.shape[0], weight.shape[0]), jnp.float32)
    for part_index in range(N_MP):
        term = jnp.dot(left[:, part_index * half:(part_index + 1) * half], weight[:, part_index * half:(part_index + 1) * half].T, preferred_element_type=jnp.float32)
        term = lax.optimization_barrier(term.astype(jnp.bfloat16))
        total = total + term.astype(jnp.float32)
    return total

def reference(hidden_in, depth, destination, weight, cotangent):
    state = hidden_in
    levels = depth
    saved = []
    for step in range(3):
        state = jnp.zeros_like(state).at[destination[step]].set(state)
        levels = jnp.zeros_like(levels).at[destination[step]].set(levels)
        state_f = state.astype(jnp.float32)
        rinv = lax.rsqrt(lax.optimization_barrier(jnp.mean(state_f * state_f, axis=-1, keepdims=True)) + 1e-06)
        normed = (state_f * rinv).astype(jnp.bfloat16)
        inner = jnp.dot(normed, weight, preferred_element_type=jnp.float32)
        gated = jax.nn.silu(inner).astype(jnp.bfloat16)
        branch = halves_product(gated, weight)
        active = (levels >= step + 1).astype(jnp.float32)[:, None]
        saved.append((state_f, rinv, normed, inner, gated, active))
        state = (state_f + active * branch).astype(jnp.bfloat16)
    final = state
    grad_state = cotangent.astype(jnp.float32)
    grad_weight = jnp.zeros((D, INNER), jnp.float32)
    for step in (2, 1, 0):
        state_f, rinv, normed, inner, gated, active = saved[step]
        grad_branch = (active * grad_state).astype(jnp.bfloat16)
        grad_gated = jnp.dot(grad_branch, weight, preferred_element_type=jnp.float32)
        sigma = jax.nn.sigmoid(inner)
        grad_inner = (grad_gated * sigma * (1.0 + inner * (1.0 - sigma))).astype(jnp.bfloat16)
        grad_normed = halves_product(grad_inner, weight)
        inner_mean = lax.optimization_barrier(jnp.mean(grad_normed * state_f, axis=-1, keepdims=True))
        grad_entry = grad_state + rinv * grad_normed - state_f * rinv * rinv * rinv * inner_mean
        grad_weight = grad_weight + jnp.dot(normed.T, grad_inner, preferred_element_type=jnp.float32) + jnp.dot(grad_branch.T, gated, preferred_element_type=jnp.float32)
        grad_state = grad_entry.astype(jnp.bfloat16)[destination[step]].astype(jnp.float32)
    return (final, grad_state.astype(jnp.bfloat16), grad_weight)
```

```python
import jax
import jax.numpy as jnp
from jax import lax
from jax.sharding import Mesh, PartitionSpec as P

DP = ("x", "z", "y", "c")
RING = ("m", "z")
BF = jnp.bfloat16
F32 = jnp.float32
NN = (((1,), (0,)), ((), ()))
NT = (((1,), (1,)), ((), ()))
TN = (((0,), (0,)), ((), ()))


def mm(a, b, dims=NN):
    return lax.dot_general(a, b, dims, preferred_element_type=F32)


def pick(sel, rows, dims=NN):
    return mm(sel.astype(BF), rows, dims).astype(BF)


def position(axis):
    if axis == RING:
        return lax.axis_index("m") * lax.axis_size("z") + lax.axis_index("z")
    return lax.axis_index(axis)


def shift(value, axis, k):
    n = lax.axis_size(axis)
    if axis == RING:
        nm, nz = lax.axis_size("m"), lax.axis_size("z")
        order = [(q % nz) * nm + q // nz for q in range(n)]
        return lax.ppermute(value, ("z", "m"), [(order[q], order[(q + k) % n]) for q in range(n)])
    return lax.ppermute(value, axis, [(i, (i + k) % n) for i in range(n)])


def swap(value, axis):
    return shift(value, axis, 1)


def exchange(buf):
    return lax.all_to_all(buf, DP, split_axis=0, concat_axis=0, tiled=True)


def ring_gather(block, axis):
    n = lax.axis_size(axis)
    me = position(axis)
    out = jnp.zeros((n,) + block.shape, block.dtype)
    out = lax.dynamic_update_index_in_dim(out, block, me, 0)
    for k in range(1, n):
        got = shift(block, axis, k)
        out = lax.dynamic_update_index_in_dim(out, got, (me - k + n) % n, 0)
    return out


def ring_scatter(parts, axis):
    n = lax.axis_size(axis)
    me = position(axis)
    total = lax.dynamic_index_in_dim(parts, me, 0, keepdims=False).astype(F32)
    for k in range(1, n):
        piece = lax.dynamic_index_in_dim(parts, (me + k) % n, 0, keepdims=False)
        total = total + shift(piece, axis, k).astype(F32)
    return total


def gather_weight(weight):
    nx, nz, ny, nm = (lax.axis_size(a) for a in ("x", "z", "y", "m"))
    rows, cols = weight.shape
    half = cols // 2
    quarter = half // 2
    c = lax.axis_index("c")
    mine = lax.dynamic_slice_in_dim(weight, c * half, half, 1)
    other = lax.dynamic_slice_in_dim(weight, (1 - c) * half, half, 1)
    got = swap(other, "c")
    block = jnp.zeros((2, rows, half), BF)
    block = lax.dynamic_update_index_in_dim(block, mine, c, 0)
    block = lax.dynamic_update_index_in_dim(block, got, 1 - c, 0)
    block = block.reshape(2 * rows, half)
    ring = ring_gather(block, RING)
    part0 = ring_gather(ring[:, :, :quarter], "x")
    part1 = ring_gather(ring[:, :, quarter:], "y")
    part0 = ring_gather(part0, "y")
    part1 = ring_gather(part1, "x")
    own = jnp.stack([part0.swapaxes(0, 1), part1], axis=0)
    theirs = swap(own, "c")
    both = jnp.zeros((2,) + own.shape, BF)
    both = lax.dynamic_update_index_in_dim(both, own, c, 0)
    both = lax.dynamic_update_index_in_dim(both, theirs, 1 - c, 0)
    both = both.reshape(2, 2, nx, ny, nm, nz, 2 * rows, quarter)
    full = both.transpose(2, 5, 3, 6, 4, 0, 1, 7)
    return full.reshape(nx * nz * ny * 2 * rows, nm * cols)


def scatter_weight(left, right):
    nx, nz, ny, nm = (lax.axis_size(a) for a in ("x", "z", "y", "m"))
    c = lax.axis_index("c")
    inner = right.shape[1]
    half = inner // (2 * nm)
    quarter = half // 2
    split = right.reshape(-1, nm, 2, half)
    mine = lax.dynamic_index_in_dim(split, c, 2, keepdims=False)
    other = lax.dynamic_index_in_dim(split, 1 - c, 2, keepdims=False)
    left_all = jnp.concatenate([left, swap(left, "c")], axis=0)
    right_all = jnp.concatenate([mine, swap(other, "c")], axis=0)
    d = left.shape[1]
    rows = d // (nx * nz * ny)
    tot0 = mm(left_all, right_all[:, :, :quarter].reshape(-1, nm * quarter), TN).astype(BF)
    tot1 = mm(left_all, right_all[:, :, quarter:].reshape(-1, nm * quarter), TN).astype(BF)
    tot0 = tot0.reshape(nx, nz, ny, rows, nm, quarter)
    tot1 = tot1.reshape(nx, nz, ny, rows, nm, quarter).transpose(2, 0, 1, 3, 4, 5)
    sum0 = ring_scatter(tot0, "x").astype(BF)
    sum1 = ring_scatter(tot1, "y").astype(BF)
    sum0 = ring_scatter(sum0.transpose(1, 0, 2, 3, 4), "y")
    sum1 = ring_scatter(sum1, "x")
    tot = jnp.concatenate([sum0, sum1], axis=-1).astype(BF).transpose(2, 0, 1, 3)
    tot = ring_scatter(tot.reshape(nm * nz, rows, half), RING)
    tot = tot.reshape(2, rows // 2, half)
    keep = lax.dynamic_index_in_dim(tot, c, 0, keepdims=False)
    send = lax.dynamic_index_in_dim(tot, 1 - c, 0, keepdims=False)
    got = swap(send, "c")
    return jnp.where(c == 0, jnp.concatenate([keep, got], 1), jnp.concatenate([got, keep], 1))


def forward(x, level, w):
    saved = []
    for step in range(3):
        xf = x.astype(F32)
        rinv = lax.rsqrt(jnp.mean(xf * xf, axis=-1, keepdims=True) + 1e-06)
        nb = (xf * rinv).astype(BF)
        u = mm(nb, w)
        g = jax.nn.silu(u).astype(BF)
        y = mm(g, w, NT)
        act = (level >= step + 1).astype(F32)
        saved.append((x, nb, u, g))
        x = (xf + act * y).astype(BF)
    return x, saved


def backward(dx, level, saved, w):
    left, right = [], []
    dx = dx.astype(F32)
    for step in (2, 1, 0):
        x, nb, u, g = saved[step]
        xf = x.astype(F32)
        rinv = lax.rsqrt(jnp.mean(xf * xf, axis=-1, keepdims=True) + 1e-06)
        act = (level >= step + 1).astype(F32)
        dyb = (act * dx).astype(BF)
        s = jax.nn.sigmoid(u)
        du = (mm(dyb, w) * s * (1.0 + u * (1.0 - s))).astype(BF)
        dn = mm(du, w, NT)
        mean = jnp.mean(dn * xf, axis=-1, keepdims=True)
        left += [nb, dyb]
        right += [du, g]
        dx = (dx + rinv * dn - xf * (rinv * rinv * rinv) * mean).astype(BF).astype(F32)
    return dx.astype(BF), left, right


def body(hidden, depth, destination, weight, cotangent):
    rows, width = hidden.shape
    groups = lax.axis_size(DP)
    slots = 2 * groups
    half = width // 2
    own = rows // 2
    m = lax.axis_index("m")

    dev = destination // rows
    slot = destination % rows
    earlier = jnp.arange(rows)[:, None] > jnp.arange(rows)[None, :]
    rank = jnp.sum((dev[:, :, None] == dev[:, None, :]) & earlier[None], axis=2, dtype=jnp.int32)
    place = dev * 2 + rank
    send = place[:, None, :] == jnp.arange(slots, dtype=jnp.int32)[None, :, None]
    tag = jnp.sum(jnp.where(send, (slot + 1)[:, None, :], 0), axis=2)
    lev = jnp.sum(jnp.where(send[0], depth[None, :], 0), axis=1)
    tags = jnp.concatenate([tag, lev[None]], axis=0).astype(F32)
    tags = tags.reshape(4, groups, 2).transpose(1, 0, 2).reshape(groups, 8).astype(BF)
    tags = jnp.pad(tags, ((0, 0), (0, 120)))
    send_own = lax.dynamic_index_in_dim(send[0].reshape(groups, 2, rows), m, 1, keepdims=False)
    out_x = pick(send_own, hidden)
    in_x = exchange(jnp.concatenate([out_x, tags], axis=1))
    w = gather_weight(weight)

    tags = in_x[:, width : width + 8].astype(F32).astype(jnp.int32).reshape(groups, 4, 2)
    tag = tags[:, :3].transpose(1, 0, 2).reshape(3, slots)
    land = tag[:, None, :] == jnp.arange(1, rows + 1, dtype=jnp.int32)[None, :, None]

    first = tags[:, 0].T
    level_in = tags[:, 3].T
    valid = first > 0
    index = jnp.cumsum(valid.astype(jnp.int32), axis=1) - 1
    compact = valid[:, None, :] & (index[:, None, :] == jnp.arange(own)[None, :, None])
    slot_of = jnp.sum(jnp.where(compact, first[:, None, :], 0), axis=2)
    level_of = jnp.sum(jnp.where(compact, level_in[:, None, :], 0), axis=2)
    at = slot_of[:, :, None] == jnp.arange(1, rows + 1)[None, None, :]
    compact_own = lax.dynamic_index_in_dim(compact, m, 0, keepdims=False)
    level = lax.dynamic_index_in_dim(level_of, m, 0, keepdims=False)[:, None]
    at_both = jnp.where(m == 0, jnp.concatenate([at[0], at[1]]), jnp.concatenate([at[1], at[0]]))

    send = send.astype(BF)
    land = land.astype(BF)
    at_both = at_both.astype(BF)

    cot = lax.dynamic_slice_in_dim(cotangent, m * half, half, 1)
    buf = pick(land[2], cot, TN)
    back = exchange(buf.reshape(groups, 2, half)).reshape(slots, half)
    turn = pick(send[2], land[1])
    buf = pick(turn, back, TN)
    back = exchange(buf.reshape(groups, 2, half)).reshape(slots, half)
    both = pick(pick(at_both, send[1], NT), back)
    keep, got = both[:own], swap(both[own:], "m")
    dx = jnp.where(m == 0, jnp.concatenate([keep, got], 1), jnp.concatenate([got, keep], 1))

    x = pick(compact_own, in_x[:, :width])
    x, saved = forward(x, level, w)

    keep = lax.dynamic_slice_in_dim(x, m * half, half, 1)
    got = swap(lax.dynamic_slice_in_dim(x, (1 - m) * half, half, 1), "m")
    buf = pick(pick(send[1], at_both, NT), jnp.concatenate([keep, got], 0))
    moved = exchange(buf.reshape(groups, 2, half)).reshape(slots, half)
    buf = pick(turn, moved)
    moved = exchange(buf.reshape(groups, 2, half)).reshape(slots, half)
    keep = pick(land[2], moved)
    got = swap(keep, "m")
    final = jnp.where(m == 0, jnp.concatenate([keep, got], 1), jnp.concatenate([got, keep], 1))

    dx, left, right = backward(dx, level, saved, w)
    grad_weight = scatter_weight(jnp.concatenate(left), jnp.concatenate(right))

    back = exchange(pick(compact_own, dx, TN))
    used = jnp.any(dev[0][None, :] == jnp.arange(groups)[:, None], axis=1)
    index = jnp.cumsum(used.astype(jnp.int32)) - 1
    pack = (used[None, :] & (index[None, :] == jnp.arange(own)[:, None])).astype(BF)
    keep = pick(pack, back)
    got = swap(keep, "m")
    by_rank = send[0].reshape(groups, 2, rows)
    place0 = pick(by_rank[:, 0], pack, (((0,), (1,)), ((), ())))
    place1 = pick(by_rank[:, 1], pack, (((0,), (1,)), ((), ())))
    low = jnp.where(m == 0, keep, got)
    high = jnp.where(m == 0, got, keep)
    grad_in = pick(jnp.concatenate([place0, place1], 1), jnp.concatenate([low, high], 0))
    return final, grad_in, grad_weight


def solution(mesh):
    sizes = {128: (4, 4, 4, 2), 16: (2, 2, 2, 2)}[mesh.devices.shape[0]]
    fine = Mesh(mesh.devices.reshape(sizes + (mesh.devices.shape[1],)), DP + ("m",))
    placed = (P(DP, None), P(DP), P(None, DP), P(DP, "m"), P(DP, None))
    return jax.shard_map(
        body,
        mesh=fine,
        in_specs=placed,
        out_specs=(P(DP, None), P(DP, None), P(DP, "m")),
        check_vma=False,
    )
```

```python
import functools

import jax
import jax.numpy as jnp
from jax import lax
from jax.experimental import pallas as pl
from jax.experimental.pallas import tpu as pltpu
from jax.sharding import Mesh, PartitionSpec as P

DP = ("x", "z", "y", "c")
RING = ("m", "z")
BF = jnp.bfloat16
F32 = jnp.float32
NN = (((1,), (0,)), ((), ()))
NT = (((1,), (1,)), ((), ()))
TN = (((0,), (0,)), ((), ()))


def mm(a, b, dims=NN):
    return lax.dot_general(a, b, dims, preferred_element_type=F32)


def pick(sel, rows, dims=NN):
    return mm(sel.astype(BF), rows, dims).astype(BF)


def position(axis):
    if axis == RING:
        return lax.axis_index("m") * lax.axis_size("z") + lax.axis_index("z")
    return lax.axis_index(axis)


def shift(value, axis, k):
    n = lax.axis_size(axis)
    if axis == RING:
        nm, nz = lax.axis_size("m"), lax.axis_size("z")
        order = [(q % nz) * nm + q // nz for q in range(n)]
        return lax.ppermute(value, ("z", "m"), [(order[q], order[(q + k) % n]) for q in range(n)])
    return lax.ppermute(value, axis, [(i, (i + k) % n) for i in range(n)])


def swap(value, axis):
    return shift(value, axis, 1)


def exchange(buf):
    return lax.all_to_all(buf, DP, split_axis=0, concat_axis=0, tiled=True)


def ring_gather(block, axis, dim):
    n = lax.axis_size(axis)
    me = lax.axis_index(axis)
    out = jnp.zeros(block.shape[:dim] + (n,) + block.shape[dim:], block.dtype)
    out = lax.dynamic_update_index_in_dim(out, block, me, dim)
    for k in range(1, n):
        got = shift(block, axis, k)
        out = lax.dynamic_update_index_in_dim(out, got, (me - k + n) % n, dim)
    return out


def ring_scatter(parts, axis, dim):
    n = lax.axis_size(axis)
    me = lax.axis_index(axis)
    total = lax.dynamic_index_in_dim(parts, me, dim, keepdims=False).astype(F32)
    for k in range(1, n):
        piece = lax.dynamic_index_in_dim(parts, (me + k) % n, dim, keepdims=False)
        total = total + shift(piece, axis, k).astype(F32)
    return total


def tie(*values):
    return lax.optimization_barrier(values)


def near_weight(weight):
    half = weight.shape[1] // 2
    c, m = lax.axis_index("c"), lax.axis_index("m")
    mine = lax.dynamic_slice_in_dim(weight, c * half, half, 1)
    other = lax.dynamic_slice_in_dim(weight, (1 - c) * half, half, 1)
    got = swap(other, "c")
    block = jnp.where(c == 0, jnp.concatenate([mine, got], 0), jnp.concatenate([got, mine], 0))
    far = swap(block, "m")
    return jnp.where(m == 0, jnp.stack([block, far]), jnp.stack([far, block]))


def plane_weight(block):
    block = ring_gather(block, "z", 1)
    quarter = block.shape[-1] // 2
    near0, near1 = ring_near(block[..., :quarter], "x"), ring_near(block[..., quarter:], "y")
    return in_order(ring_rest(near0, "x"), "x", 1), in_order(ring_rest(near1, "y"), "y", 2)


def in_order(blocks, axis, dim):
    n = lax.axis_size(axis)
    me = lax.axis_index(axis)
    out = jnp.zeros(blocks[0].shape[:dim] + (n,) + blocks[0].shape[dim:], BF)
    for k, block in zip(distances(n), blocks, strict=True):
        out = lax.dynamic_update_index_in_dim(out, block, (me - k + n) % n, dim)
    return out


def onward(n):
    return [(2 * i + side, 2 * ((i + (n - 1 if side else 1)) % n) + side) for i in range(n) for side in range(2)]


def ring_near(part, axis):
    n = lax.axis_size(axis)
    return [part] + [shift(part, axis, k) for k in distances(n)[1:3]]


def ring_rest(near, axis):
    n = lax.axis_size(axis)
    if n == 2:
        return near
    far = jnp.where(lax.axis_index("c") == 0, near[1], near[2])
    return near + [lax.ppermute(far, (axis, "c"), onward(n))]


def distances(n):
    return [0, 1] if n == 2 else [0, 1, 3, 2]


def load_weight(place, pieces, w_ref, sems):
    nx, ny = w_ref.shape[3], w_ref.shape[5]
    x, y, c = place[0], place[1], place[2]
    kinds = [(0, k) for k in distances(ny)] + [(1, k) for k in distances(nx)]
    copies = {}
    for part, side in enumerate((c, 1 - c)):
        group = pieces[part * len(kinds) : (part + 1) * len(kinds)]
        for ref, (s, k) in zip(group, kinds, strict=True):
            for m in range(2):
                if s == 0:
                    goal = w_ref.at[m, side, 0, :, :, lax.rem(y - k + ny, ny)]
                else:
                    goal = w_ref.at[m, side, 1, lax.rem(x - k + nx, nx)]
                copies[part, s, m, k] = pltpu.make_async_copy(ref.at[m], goal, sems.at[part, s, m, k])
    for copy in copies.values():
        copy.start()
    return copies


def blocks_of(w_ref, place):
    nm, _, ns = w_ref.shape[:3]
    wide = w_ref.shape[-1]
    depth = 1
    for size in w_ref.shape[3:-1]:
        depth *= size
    c = place[2]
    for part, side in enumerate((c, 1 - c)):
        for s in range(ns):
            for m in range(nm):
                first = pl.multiple_of(((m * 2 + side) * ns + s) * wide, wide)
                yield (part, s, m), pl.ds(first, wide), lambda m=m, side=side, s=s: w_ref[m, side, s].reshape(depth, wide)


def arrived(copies, key):
    part, s, m = key
    for name, copy in copies.items():
        if name[:3] == (part, s, m):
            copy.wait()


def norm(x):
    xf = x.astype(F32)
    rinv = lax.rsqrt(jnp.mean(xf * xf, axis=-1, keepdims=True) + 1e-06)
    return xf, rinv


def forward_kernel(n, place, level, x_ref, *refs):
    pieces = refs[:n]
    final, xs, nbs, us, g_own, g_other, w_ref, g_ref, acc, sems = refs[n:]
    copies = load_weight(place, pieces, w_ref, sems)
    rows, wide = x_ref.shape[0], w_ref.shape[-1]
    x = x_ref[...]
    for step in range(3):
        own = pl.ds(step * rows, rows)
        xf, rinv = norm(x)
        nb = (xf * rinv).astype(BF)
        xs[step] = x
        nbs[own, :] = nb
        for key, cols, block in blocks_of(w_ref, place):
            if step == 0:
                arrived(copies, key)
            part, s, m = key
            u = mm(nb, block())
            us[step, :, cols] = u
            g = jax.nn.silu(u).astype(BF)
            g_ref[:, cols] = g
            out = g_other if part else g_own
            out[own, (s * 2 + m) * wide : (s * 2 + m + 1) * wide] = g
        total = None
        for key, cols, block in blocks_of(w_ref, place):
            term = mm(g_ref[:, cols], block(), NT)
            total = term if total is None else total + term
        act = (level[...] >= step + 1).astype(F32)
        x = (xf + act * total).astype(BF)
    final[...] = x


def backward_kernel(n, place, level, dx_ref, xs, us, *refs):
    pieces = refs[:n]
    dx_out, dybs, du_own, du_other, w_ref, du_ref, acc, sems = refs[n:]
    copies = load_weight(place, pieces, w_ref, sems)
    rows, wide = dx_ref.shape[0], w_ref.shape[-1]
    dx = dx_ref[...].astype(F32)
    for step in (2, 1, 0):
        own = pl.ds(step * rows, rows)
        act = (level[...] >= step + 1).astype(F32)
        dyb = (act * dx).astype(BF)
        dybs[own, :] = dyb
        for key, cols, block in blocks_of(w_ref, place):
            if step == 2:
                arrived(copies, key)
            part, s, m = key
            u = us[step, :, cols]
            sig = jax.nn.sigmoid(u)
            du = (mm(dyb, block()) * sig * (1.0 + u * (1.0 - sig))).astype(BF)
            du_ref[:, cols] = du
            out = du_other if part else du_own
            out[own, (s * 2 + m) * wide : (s * 2 + m + 1) * wide] = du
        dn = None
        for key, cols, block in blocks_of(w_ref, place):
            term = mm(du_ref[:, cols], block(), NT)
            dn = term if dn is None else dn + term
        xf, rinv = norm(xs[step])
        mean = jnp.mean(dn * xf, axis=-1, keepdims=True)
        dx = (dx + rinv * dn - xf * (rinv * rinv * rinv) * mean).astype(BF).astype(F32)
    dx_out[...] = dx.astype(BF)


def block_call(kernel, name, place, pieces, operands, outs, dims):
    nx, nz, ny, rows, wide = dims
    count, width = operands[1].shape
    vmem = pl.BlockSpec(memory_space=pltpu.VMEM)
    work = 36 * count * width * width
    return pl.pallas_call(
        functools.partial(kernel, len(pieces)),
        out_shape=outs,
        in_specs=[pl.BlockSpec(memory_space=pltpu.SMEM)]
        + [vmem] * len(operands)
        + [pl.BlockSpec(memory_space=pl.ANY)] * len(pieces),
        out_specs=[vmem] * len(outs),
        scratch_shapes=[
            pltpu.VMEM((2, 2, 2, nx, nz, ny, rows, wide), BF),
            pltpu.VMEM((count, width), BF),
            pltpu.VMEM((count, width), F32),
            pltpu.SemaphoreType.DMA((2, 2, 2, max(nx, ny))),
        ],
        compiler_params=pltpu.CompilerParams(vmem_limit_bytes=60 * 2**20),
        cost_estimate=pl.CostEstimate(flops=work, bytes_accessed=12 * 2**20, transcendentals=0),
        name=name,
    )(place, *operands, *pieces)


def product_kernel(place, *refs):
    sources, outs, (left, right, tot0, tot1, sems, out_sems) = refs[:8], refs[8:-6], refs[-6:]
    rows = sources[0].shape[0]
    nx, nz, ny, row, wide = tot0.shape
    copies = []
    for i in range(4):
        copies.append(pltpu.make_async_copy(sources[i], left.at[pl.ds(i * rows, rows)], sems.at[i]))
        copies.append(pltpu.make_async_copy(sources[4 + i], right.at[pl.ds(i * rows, rows)], sems.at[4 + i]))
    for copy in copies:
        copy.start()
    for copy in copies:
        copy.wait()
    chunk = left.shape[1] // nx
    for k in range(nx):
        full = mm(left[:, k * chunk : (k + 1) * chunk], right[...], TN).astype(BF)
        tot0[k] = full[:, :wide].reshape(nz, ny, row, wide)
        part = full[:, wide:].reshape(nz, ny, row, wide)
        for y in range(ny):
            tot1[y, k] = part[:, y]
    copies = []
    for t in range(nx):
        copies.append(pltpu.make_async_copy(tot0.at[lax.rem(place[0] + t, nx)], outs[t], out_sems.at[t]))
    for t in range(ny):
        copies.append(pltpu.make_async_copy(tot1.at[lax.rem(place[1] + t, ny)], outs[nx + t], out_sems.at[nx + t]))
    for copy in copies:
        copy.start()
    for copy in copies:
        copy.wait()


def product_call(place, sources, dims):
    nx, nz, ny, row, wide = dims
    rows, width = sources[0].shape
    outs = [jax.ShapeDtypeStruct((nz, ny, row, 2 * wide), BF)] * nx
    outs += [jax.ShapeDtypeStruct((nx, nz, row, 2 * wide), BF)] * ny
    outs = pl.pallas_call(
        product_kernel,
        out_shape=outs,
        in_specs=[pl.BlockSpec(memory_space=pltpu.SMEM)] + [pl.BlockSpec(memory_space=pl.ANY)] * 8,
        out_specs=[pl.BlockSpec(memory_space=pl.ANY)] * (nx + ny),
        scratch_shapes=[
            pltpu.VMEM((4 * rows, width), BF),
            pltpu.VMEM((4 * rows, 4 * wide), BF),
            pltpu.VMEM((nx, nz, ny, row, 2 * wide), BF),
            pltpu.VMEM((ny, nx, nz, row, 2 * wide), BF),
            pltpu.SemaphoreType.DMA((8,)),
            pltpu.SemaphoreType.DMA((nx + ny,)),
        ],
        compiler_params=pltpu.CompilerParams(vmem_limit_bytes=60 * 2**20),
        cost_estimate=pl.CostEstimate(flops=96 * rows * width * wide, bytes_accessed=9 * 2**20, transcendentals=0),
        name="products",
    )(place, *sources)
    return outs[:nx], outs[nx:]


def sum_first(groups, after):
    c = lax.axis_index("c")
    near = []
    for axis, pieces in zip(("x", "y"), groups, strict=True):
        if len(pieces) == 4:
            far = lax.ppermute(pieces[2], (axis, "c"), onward(4)).astype(F32)
            up = (pieces[1].astype(F32) + jnp.where(c == 0, far, 0.0)).astype(BF)
            down = (pieces[3].astype(F32) + jnp.where(c == 0, 0.0, far)).astype(BF)
            near.append([pieces[0], shift(up, axis, 1), shift(down, axis, 3)])
        else:
            near.append([pieces[0], shift(pieces[1], axis, 1)])
    near, _ = tie(near, after)
    return [sum((piece.astype(F32) for piece in others), mine.astype(F32)).astype(BF) for mine, *others in near]


def sum_second(sum0, sum1):
    return ring_scatter(sum0, "y", 1).astype(BF), ring_scatter(sum1, "x", 0).astype(BF)


def sum_line(sum0, sum1):
    nz, row, wide = sum0.shape
    m = lax.axis_index("m")
    tot = jnp.concatenate([sum0.reshape(nz, row, 2, wide // 2), sum1.reshape(nz, row, 2, wide // 2)], axis=-1)
    tot = ring_scatter(tot, "z", 0).astype(BF)
    keep = lax.dynamic_index_in_dim(tot, m, 1, keepdims=False)
    send = lax.dynamic_index_in_dim(tot, 1 - m, 1, keepdims=False)
    return keep.astype(F32) + swap(send, "m").astype(F32)


def sum_cores(total):
    c = lax.axis_index("c")
    total = total.reshape(2, -1, total.shape[-1])
    keep = lax.dynamic_index_in_dim(total, c, 0, keepdims=False)
    send = lax.dynamic_index_in_dim(total, 1 - c, 0, keepdims=False)
    got = swap(send, "c")
    return jnp.where(c == 0, jnp.concatenate([keep, got], 1), jnp.concatenate([got, keep], 1))


def body(hidden, depth, destination, weight, cotangent):
    rows, width = hidden.shape
    groups = lax.axis_size(DP)
    slots = 2 * groups
    half = width // 2
    own = rows // 2
    m = lax.axis_index("m")

    dev = destination // rows
    slot = destination % rows
    earlier = jnp.arange(rows)[:, None] > jnp.arange(rows)[None, :]
    rank = jnp.sum((dev[:, :, None] == dev[:, None, :]) & earlier[None], axis=2, dtype=jnp.int32)
    place = dev * 2 + rank
    send = place[:, None, :] == jnp.arange(slots, dtype=jnp.int32)[None, :, None]
    tag = jnp.sum(jnp.where(send, (slot + 1)[:, None, :], 0), axis=2)
    lev = jnp.sum(jnp.where(send[0], depth[None, :], 0), axis=1)
    tags = jnp.concatenate([tag, lev[None]], axis=0).astype(F32)
    tags = tags.reshape(4, groups, 2).transpose(1, 0, 2).reshape(groups, 8).astype(BF)
    tags = jnp.pad(tags, ((0, 0), (0, 120)))
    send_own = lax.dynamic_index_in_dim(send[0].reshape(groups, 2, rows), m, 1, keepdims=False)
    out_x = pick(send_own, hidden)
    buf = jnp.concatenate([out_x, tags], axis=1).reshape(groups, 2, -1)
    block, buf = tie(near_weight(weight), buf)
    in_x = exchange(buf).reshape(groups, -1)
    part0, part1 = plane_weight(block)
    nx, nz, ny = lax.axis_size("x"), lax.axis_size("z"), lax.axis_size("y")
    dims = (nx, nz, ny, 2 * weight.shape[0], weight.shape[1] // 4)
    here = jnp.stack([lax.axis_index("x"), lax.axis_index("y"), lax.axis_index("c")]).astype(jnp.int32)
    shape = jax.ShapeDtypeStruct

    tags = in_x[:, width : width + 8].astype(F32).astype(jnp.int32).reshape(groups, 4, 2)
    tag = tags[:, :3].transpose(1, 0, 2).reshape(3, slots)
    land = tag[:, None, :] == jnp.arange(1, rows + 1, dtype=jnp.int32)[None, :, None]

    first = tags[:, 0].T
    level_in = tags[:, 3].T
    valid = first > 0
    index = jnp.cumsum(valid.astype(jnp.int32), axis=1) - 1
    compact = valid[:, None, :] & (index[:, None, :] == jnp.arange(own)[None, :, None])
    slot_of = jnp.sum(jnp.where(compact, first[:, None, :], 0), axis=2)
    level_of = jnp.sum(jnp.where(compact, level_in[:, None, :], 0), axis=2)
    at = slot_of[:, :, None] == jnp.arange(1, rows + 1)[None, None, :]
    compact_own = lax.dynamic_index_in_dim(compact, m, 0, keepdims=False)
    level = lax.dynamic_index_in_dim(level_of, m, 0, keepdims=False)[:, None]
    at_both = jnp.where(m == 0, jnp.concatenate([at[0], at[1]]), jnp.concatenate([at[1], at[0]]))

    send = send.astype(BF)
    land = land.astype(BF)
    at_both = at_both.astype(BF)

    cot = lax.dynamic_slice_in_dim(cotangent, m * half, half, 1)
    buf = pick(land[2], cot, TN).reshape(groups, 2, half)
    part0, part1, buf = tie(part0, part1, buf)
    near0, near1 = ring_near(part0, "y"), ring_near(part1, "x")
    pieces = ring_rest(near0, "y") + ring_rest(near1, "x")
    back = exchange(buf).reshape(slots, half)
    turn = pick(send[2], land[1])
    buf = pick(turn, back, TN).reshape(groups, 2, half)
    *pieces, buf = tie(*pieces, buf)
    pieces = pieces + [swap(piece, "c") for piece in pieces]
    back = exchange(buf).reshape(slots, half)

    x = pick(compact_own, in_x[:, :width])
    x, xs, nbs, us, g_own, g_other = block_call(
        forward_kernel, "forward", here, pieces, (level, x),
        [
            shape((own, width), BF),
            shape((3, own, width), BF),
            shape((3 * own, width), BF),
            shape((3, own, width), F32),
            shape((3 * own, half), BF),
            shape((3 * own, half), BF),
        ],
        dims,
    )
    nbs_far, g_far = swap(nbs, "c"), swap(g_other, "c")
    us, back = tie(us, back)
    both = pick(pick(at_both, send[1], NT), back)
    keep, got = both[:own], swap(both[own:], "m")
    dx = jnp.where(m == 0, jnp.concatenate([keep, got], 1), jnp.concatenate([got, keep], 1))

    x, _ = tie(x, got)
    state = lax.dynamic_slice_in_dim(x, m * half, half, 1)
    state_far = swap(lax.dynamic_slice_in_dim(x, (1 - m) * half, half, 1), "m")

    dx, dybs, du_own, du_other = block_call(
        backward_kernel, "backward", here, pieces, (level, dx, xs, us),
        [
            shape((own, width), BF),
            shape((3 * own, width), BF),
            shape((3 * own, half), BF),
            shape((3 * own, half), BF),
        ],
        dims,
    )
    buf = pick(pick(send[1], at_both, NT), jnp.concatenate([state, state_far], 0)).reshape(groups, 2, half)
    buf = jnp.concatenate([buf, pick(compact_own, dx, TN).reshape(groups, 2, half)], 1)
    dybs, du_own, du_other, buf = tie(dybs, du_own, du_other, buf)
    dybs_far, du_far = swap(dybs, "c"), swap(du_other, "c")
    moved = exchange(buf)
    back = moved[:, 2:].reshape(groups, width)
    buf = pick(turn, moved[:, :2].reshape(slots, half)).reshape(groups, 2, half)
    moved = exchange(buf).reshape(slots, half)

    sources = [nbs, nbs_far, dybs, dybs_far, du_own, du_far, g_own, g_far]
    used = jnp.any(dev[0][None, :] == jnp.arange(groups)[:, None], axis=1)
    index = jnp.cumsum(used.astype(jnp.int32)) - 1
    pack = (used[None, :] & (index[None, :] == jnp.arange(own)[:, None])).astype(BF)
    grad_keep = pick(pack, back)
    grad_got = swap(grad_keep, "m")
    sum0, sum1 = sum_first(product_call(here, sources, dims), (buf, grad_got))
    sum0, sum1 = sum_second(sum0, sum1)
    keep = pick(land[2], moved)
    got = swap(keep, "m")
    sum0, sum1, keep = tie(sum0, sum1, keep)
    total = sum_line(sum0, sum1)
    grad_weight = sum_cores(total)
    final = jnp.where(m == 0, jnp.concatenate([keep, got], 1), jnp.concatenate([got, keep], 1))

    by_rank = send[0].reshape(groups, 2, rows)
    place0 = pick(by_rank[:, 0], pack, (((0,), (1,)), ((), ())))
    place1 = pick(by_rank[:, 1], pack, (((0,), (1,)), ((), ())))
    low = jnp.where(m == 0, grad_keep, grad_got)
    high = jnp.where(m == 0, grad_got, grad_keep)
    grad_in = pick(jnp.concatenate([place0, place1], 1), jnp.concatenate([low, high], 0))
    return final, grad_in, grad_weight


def solution(mesh):
    sizes = {128: (4, 4, 4, 2), 16: (2, 2, 2, 2)}[mesh.devices.shape[0]]
    fine = Mesh(mesh.devices.reshape(sizes + (mesh.devices.shape[1],)), DP + ("m",))
    placed = (P(DP, None), P(DP), P(None, DP), P(DP, "m"), P(DP, None))
    return jax.shard_map(
        body,
        mesh=fine,
        in_specs=placed,
        out_specs=(P(DP, None), P(DP, None), P(DP, "m")),
        check_vma=False,
    )
```

```python
import functools

import jax
import jax.numpy as jnp
from jax import lax
from jax.experimental import pallas as pl
from jax.experimental.pallas import tpu as pltpu
from jax.sharding import Mesh, PartitionSpec as P

DP = ("x", "z", "y", "c")
RING = ("m", "z")
BF = jnp.bfloat16
F32 = jnp.float32
NN = (((1,), (0,)), ((), ()))
NT = (((1,), (1,)), ((), ()))
TN = (((0,), (0,)), ((), ()))


def mm(a, b, dims=NN):
    return lax.dot_general(a, b, dims, preferred_element_type=F32)


def pick(sel, rows, dims=NN):
    return mm(sel.astype(BF), rows, dims).astype(BF)


def position(axis):
    if axis == RING:
        return lax.axis_index("m") * lax.axis_size("z") + lax.axis_index("z")
    return lax.axis_index(axis)


def shift(value, axis, k):
    n = lax.axis_size(axis)
    if axis == RING:
        nm, nz = lax.axis_size("m"), lax.axis_size("z")
        order = [(q % nz) * nm + q // nz for q in range(n)]
        return lax.ppermute(value, ("z", "m"), [(order[q], order[(q + k) % n]) for q in range(n)])
    return lax.ppermute(value, axis, [(i, (i + k) % n) for i in range(n)])


def swap(value, axis):
    return shift(value, axis, 1)


def exchange(buf):
    return lax.all_to_all(buf, DP, split_axis=0, concat_axis=0, tiled=True)


def ring_gather(block, axis, dim):
    n = lax.axis_size(axis)
    me = lax.axis_index(axis)
    out = jnp.zeros(block.shape[:dim] + (n,) + block.shape[dim:], block.dtype)
    out = lax.dynamic_update_index_in_dim(out, block, me, dim)
    for k in range(1, n):
        got = shift(block, axis, k)
        out = lax.dynamic_update_index_in_dim(out, got, (me - k + n) % n, dim)
    return out


def ring_scatter(parts, axis, dim):
    n = lax.axis_size(axis)
    me = lax.axis_index(axis)
    total = lax.dynamic_index_in_dim(parts, me, dim, keepdims=False).astype(F32)
    for k in range(1, n):
        piece = lax.dynamic_index_in_dim(parts, (me + k) % n, dim, keepdims=False)
        total = total + shift(piece, axis, k).astype(F32)
    return total


def tie(*values):
    return lax.optimization_barrier(values)


def near_weight(weight):
    half = weight.shape[1] // 2
    c, m = lax.axis_index("c"), lax.axis_index("m")
    mine = lax.dynamic_slice_in_dim(weight, c * half, half, 1)
    other = lax.dynamic_slice_in_dim(weight, (1 - c) * half, half, 1)
    got = swap(other, "c")
    block = jnp.where(c == 0, jnp.concatenate([mine, got], 0), jnp.concatenate([got, mine], 0))
    far = swap(block, "m")
    return jnp.where(m == 0, jnp.stack([block, far]), jnp.stack([far, block]))


def plane_weight(block):
    block = ring_gather(block, "z", 1)
    quarter = block.shape[-1] // 2
    near0, near1 = ring_near(block[..., :quarter], "x"), ring_near(block[..., quarter:], "y")
    return in_order(ring_rest(near0, "x"), "x", 1), in_order(ring_rest(near1, "y"), "y", 2)


def in_order(blocks, axis, dim):
    n = lax.axis_size(axis)
    me = lax.axis_index(axis)
    out = jnp.zeros(blocks[0].shape[:dim] + (n,) + blocks[0].shape[dim:], BF)
    for k, block in zip(distances(n), blocks, strict=True):
        out = lax.dynamic_update_index_in_dim(out, block, (me - k + n) % n, dim)
    return out


def onward(n):
    return [(2 * i + side, 2 * ((i + (n - 1 if side else 1)) % n) + side) for i in range(n) for side in range(2)]


def ring_near(part, axis):
    n = lax.axis_size(axis)
    return [part] + [shift(part, axis, k) for k in distances(n)[1:3]]


def ring_rest(near, axis):
    n = lax.axis_size(axis)
    if n == 2:
        return near
    far = jnp.where(lax.axis_index("c") == 0, near[1], near[2])
    return near + [lax.ppermute(far, (axis, "c"), onward(n))]


def distances(n):
    return [0, 1] if n == 2 else [0, 1, 3, 2]


def load_weight(place, pieces, w_ref, sems):
    nx, ny = w_ref.shape[3], w_ref.shape[5]
    x, y, c = place[0], place[1], place[2]
    kinds = [(0, k) for k in distances(ny)] + [(1, k) for k in distances(nx)]
    copies = {}
    for part, side in enumerate((c, 1 - c)):
        group = pieces[part * len(kinds) : (part + 1) * len(kinds)]
        for ref, (s, k) in zip(group, kinds, strict=True):
            for m in range(2):
                if s == 0:
                    goal = w_ref.at[m, side, 0, :, :, lax.rem(y - k + ny, ny)]
                else:
                    goal = w_ref.at[m, side, 1, lax.rem(x - k + nx, nx)]
                copies[part, s, m, k] = pltpu.make_async_copy(ref.at[m], goal, sems.at[part, s, m, k])
    for copy in copies.values():
        copy.start()
    return copies


def blocks_of(w_ref, place):
    nm, _, ns = w_ref.shape[:3]
    wide = w_ref.shape[-1]
    depth = 1
    for size in w_ref.shape[3:-1]:
        depth *= size
    c = place[2]
    for part, side in enumerate((c, 1 - c)):
        for s in range(ns):
            for m in range(nm):
                first = pl.multiple_of(((m * 2 + side) * ns + s) * wide, wide)
                yield (part, s, m), pl.ds(first, wide), lambda m=m, side=side, s=s: w_ref[m, side, s].reshape(depth, wide)


def arrived(copies, key):
    part, s, m = key
    for name, copy in copies.items():
        if name[:3] == (part, s, m):
            copy.wait()


def norm(x):
    xf = x.astype(F32)
    rinv = lax.rsqrt(jnp.mean(xf * xf, axis=-1, keepdims=True) + 1e-06)
    return xf, rinv


def times_turned(left, wt_ref, parts, store):
    count = wt_ref.shape[1] // parts
    for k in range(parts):
        at = slice(k * count, (k + 1) * count)
        store(at, mm(left, wt_ref[:, at]))


def forward_kernel(n, place, level, x_ref, *refs):
    pieces = refs[:n]
    final, xs, nbs, slopes, g_own, g_other, turned, w_ref, wt_ref, g_ref, y_ref, sems, turn_sem = refs[n:]
    copies = load_weight(place, pieces, w_ref, sems)
    rows, wide = x_ref.shape[0], w_ref.shape[-1]
    x = x_ref[...]
    for step in range(3):
        own = pl.ds(step * rows, rows)
        xf, rinv = norm(x)
        nb = (xf * rinv).astype(BF)
        xs[step] = x
        nbs[own, :] = nb
        for key, cols, block in blocks_of(w_ref, place):
            if step == 0:
                arrived(copies, key)
            part, s, m = key
            w = block()
            if step == 0:
                wt_ref[cols, :] = w.T
            u = mm(nb, w)
            sig = jax.nn.sigmoid(u)
            slopes[step, :, cols] = sig * (1.0 + u * (1.0 - sig))
            g = (u * sig).astype(BF)
            g_ref[:, cols] = g
            out = g_other if part else g_own
            out[own, (s * 2 + m) * wide : (s * 2 + m + 1) * wide] = g
        act = (level[...] >= step + 1).astype(F32)

        def store(at, y, step=step, act=act):
            y_ref[:, at] = (xs[step, :, at].astype(F32) + act * y).astype(BF)

        if step == 0:
            copy = pltpu.make_async_copy(wt_ref, turned, turn_sem)
            copy.start()
        times_turned(g_ref[...], wt_ref, 4, store)
        x = y_ref[...]
    final[...] = x
    copy.wait()


def backward_kernel(n, place, level, dx_ref, xs, slopes, *refs):
    pieces, turned = refs[:n], refs[n]
    dx_out, dybs, du_own, du_other, w_ref, wt_ref, du_ref, dn_ref, sems, turn_sem = refs[n + 1 :]
    copies = load_weight(place, pieces, w_ref, sems)
    copy = pltpu.make_async_copy(turned, wt_ref, turn_sem)
    copy.start()
    rows, wide = dx_ref.shape[0], w_ref.shape[-1]
    dx_out[...] = dx_ref[...]
    for step in (2, 1, 0):
        own = pl.ds(step * rows, rows)
        act = (level[...] >= step + 1).astype(F32)
        dyb = (act * dx_out[...].astype(F32)).astype(BF)
        dybs[own, :] = dyb
        for key, cols, block in blocks_of(w_ref, place):
            if step == 2:
                arrived(copies, key)
            part, s, m = key
            du = (mm(dyb, block()) * slopes[step, :, cols]).astype(BF)
            du_ref[:, cols] = du
            out = du_other if part else du_own
            out[own, (s * 2 + m) * wide : (s * 2 + m + 1) * wide] = du

        def store(at, dn):
            dn_ref[:, at] = dn

        if step == 2:
            copy.wait()
        times_turned(du_ref[...], wt_ref, 4, store)
        xf, rinv = norm(xs[step])
        dn = dn_ref[...]
        mean = jnp.mean(dn * xf, axis=-1, keepdims=True)
        dx = dx_out[...].astype(F32) + rinv * dn - xf * (rinv * rinv * rinv) * mean
        dx_out[...] = dx.astype(BF)


def block_call(kernel, name, place, pieces, operands, outs, last, dims):
    nx, nz, ny, rows, wide = dims
    count, width = operands[1].shape
    vmem = pl.BlockSpec(memory_space=pltpu.VMEM)
    work = 36 * count * width * width
    return pl.pallas_call(
        functools.partial(kernel, 4 * (len(distances(nx)) + len(distances(ny))) // 2),
        out_shape=outs,
        in_specs=[pl.BlockSpec(memory_space=pltpu.SMEM)]
        + [vmem] * len(operands)
        + [pl.BlockSpec(memory_space=pl.ANY)] * len(pieces),
        out_specs=[vmem if out.shape != (width, width) else pl.BlockSpec(memory_space=pl.ANY) for out in outs],
        scratch_shapes=[
            pltpu.VMEM((2, 2, 2, nx, nz, ny, rows, wide), BF),
            pltpu.VMEM((width, width), BF),
            pltpu.VMEM((count, width), BF),
            pltpu.VMEM((count, width), last),
            pltpu.SemaphoreType.DMA((2, 2, 2, max(nx, ny))),
            pltpu.SemaphoreType.DMA,
        ],
        compiler_params=pltpu.CompilerParams(vmem_limit_bytes=60 * 2**20),
        cost_estimate=pl.CostEstimate(flops=work, bytes_accessed=12 * 2**20, transcendentals=0),
        name=name,
    )(place, *operands, *pieces)


def product_kernel(place, *refs):
    sources, outs, (left, right, tot0, tot1, sems, out_sems) = refs[:8], refs[8:-6], refs[-6:]
    rows = sources[0].shape[0]
    nx, nz, ny, row, wide = tot0.shape
    copies = []
    for i in range(4):
        copies.append(pltpu.make_async_copy(sources[i], left.at[pl.ds(i * rows, rows)], sems.at[i]))
        copies.append(pltpu.make_async_copy(sources[4 + i], right.at[pl.ds(i * rows, rows)], sems.at[4 + i]))
    for copy in copies:
        copy.start()
    for copy in copies:
        copy.wait()
    chunk = left.shape[1] // nx
    for k in range(nx):
        full = mm(left[:, k * chunk : (k + 1) * chunk], right[...], TN).astype(BF)
        tot0[k] = full[:, :wide].reshape(nz, ny, row, wide)
        part = full[:, wide:].reshape(nz, ny, row, wide)
        for y in range(ny):
            tot1[y, k] = part[:, y]
    copies = []
    for t in range(nx):
        copies.append(pltpu.make_async_copy(tot0.at[lax.rem(place[0] + t, nx)], outs[t], out_sems.at[t]))
    for t in range(ny):
        copies.append(pltpu.make_async_copy(tot1.at[lax.rem(place[1] + t, ny)], outs[nx + t], out_sems.at[nx + t]))
    for copy in copies:
        copy.start()
    for copy in copies:
        copy.wait()


def product_call(place, sources, dims):
    nx, nz, ny, row, wide = dims
    rows, width = sources[0].shape
    outs = [jax.ShapeDtypeStruct((nz, ny, row, 2 * wide), BF)] * nx
    outs += [jax.ShapeDtypeStruct((nx, nz, row, 2 * wide), BF)] * ny
    outs = pl.pallas_call(
        product_kernel,
        out_shape=outs,
        in_specs=[pl.BlockSpec(memory_space=pltpu.SMEM)] + [pl.BlockSpec(memory_space=pl.ANY)] * 8,
        out_specs=[pl.BlockSpec(memory_space=pl.ANY)] * (nx + ny),
        scratch_shapes=[
            pltpu.VMEM((4 * rows, width), BF),
            pltpu.VMEM((4 * rows, 4 * wide), BF),
            pltpu.VMEM((nx, nz, ny, row, 2 * wide), BF),
            pltpu.VMEM((ny, nx, nz, row, 2 * wide), BF),
            pltpu.SemaphoreType.DMA((8,)),
            pltpu.SemaphoreType.DMA((nx + ny,)),
        ],
        compiler_params=pltpu.CompilerParams(vmem_limit_bytes=60 * 2**20),
        cost_estimate=pl.CostEstimate(flops=96 * rows * width * wide, bytes_accessed=9 * 2**20, transcendentals=0),
        name="products",
    )(place, *sources)
    return outs[:nx], outs[nx:]


def sum_first(groups, after):
    c = lax.axis_index("c")
    near = []
    for axis, pieces in zip(("x", "y"), groups, strict=True):
        if len(pieces) == 4:
            far = lax.ppermute(pieces[2], (axis, "c"), onward(4)).astype(F32)
            up = (pieces[1].astype(F32) + jnp.where(c == 0, far, 0.0)).astype(BF)
            down = (pieces[3].astype(F32) + jnp.where(c == 0, 0.0, far)).astype(BF)
            near.append([pieces[0], shift(up, axis, 1), shift(down, axis, 3)])
        else:
            near.append([pieces[0], shift(pieces[1], axis, 1)])
    near, _ = tie(near, after)
    return [sum((piece.astype(F32) for piece in others), mine.astype(F32)).astype(BF) for mine, *others in near]


def sum_second(sum0, sum1):
    return ring_scatter(sum0, "y", 1).astype(BF), ring_scatter(sum1, "x", 0).astype(BF)


def sum_line(sum0, sum1):
    nz, row, wide = sum0.shape
    tot = jnp.concatenate([sum0.reshape(nz, row, 2, wide // 2), sum1.reshape(nz, row, 2, wide // 2)], axis=-1)
    return ring_scatter(tot, "z", 0).astype(BF)


def sum_ends(tot):
    m = lax.axis_index("m")
    keep = lax.dynamic_index_in_dim(tot, m, 1, keepdims=False)
    send = lax.dynamic_index_in_dim(tot, 1 - m, 1, keepdims=False)
    return keep.astype(F32) + swap(send, "m").astype(F32)


def sum_cores(total):
    c = lax.axis_index("c")
    total = total.reshape(2, -1, total.shape[-1])
    keep = lax.dynamic_index_in_dim(total, c, 0, keepdims=False)
    send = lax.dynamic_index_in_dim(total, 1 - c, 0, keepdims=False)
    got = swap(send, "c")
    return jnp.where(c == 0, jnp.concatenate([keep, got], 1), jnp.concatenate([got, keep], 1))


def body(hidden, depth, destination, weight, cotangent):
    rows, width = hidden.shape
    groups = lax.axis_size(DP)
    slots = 2 * groups
    half = width // 2
    own = rows // 2
    m = lax.axis_index("m")

    dev = destination // rows
    slot = destination % rows
    earlier = jnp.arange(rows)[:, None] > jnp.arange(rows)[None, :]
    rank = jnp.sum((dev[:, :, None] == dev[:, None, :]) & earlier[None], axis=2, dtype=jnp.int32)
    place = dev * 2 + rank
    send = place[:, None, :] == jnp.arange(slots, dtype=jnp.int32)[None, :, None]
    tag = jnp.sum(jnp.where(send, (slot + 1)[:, None, :], 0), axis=2)
    lev = jnp.sum(jnp.where(send[0], depth[None, :], 0), axis=1)
    tags = jnp.concatenate([tag, lev[None]], axis=0).astype(F32)
    tags = tags.reshape(4, groups, 2).transpose(1, 0, 2).reshape(groups, 8).astype(BF)
    tags = jnp.pad(tags, ((0, 0), (0, 120)))
    send_own = lax.dynamic_index_in_dim(send[0].reshape(groups, 2, rows), m, 1, keepdims=False)
    out_x = pick(send_own, hidden)
    buf = jnp.concatenate([out_x, tags], axis=1).reshape(groups, 2, -1)
    block, buf = tie(near_weight(weight), buf)
    in_x = exchange(buf).reshape(groups, -1)
    part0, part1 = plane_weight(block)
    nx, nz, ny = lax.axis_size("x"), lax.axis_size("z"), lax.axis_size("y")
    dims = (nx, nz, ny, 2 * weight.shape[0], weight.shape[1] // 4)
    here = jnp.stack([lax.axis_index("x"), lax.axis_index("y"), lax.axis_index("c")]).astype(jnp.int32)
    shape = jax.ShapeDtypeStruct

    tags = in_x[:, width : width + 8].astype(F32).astype(jnp.int32).reshape(groups, 4, 2)
    tag = tags[:, :3].transpose(1, 0, 2).reshape(3, slots)
    land = tag[:, None, :] == jnp.arange(1, rows + 1, dtype=jnp.int32)[None, :, None]

    first = tags[:, 0].T
    level_in = tags[:, 3].T
    valid = first > 0
    index = jnp.cumsum(valid.astype(jnp.int32), axis=1) - 1
    compact = valid[:, None, :] & (index[:, None, :] == jnp.arange(own)[None, :, None])
    slot_of = jnp.sum(jnp.where(compact, first[:, None, :], 0), axis=2)
    level_of = jnp.sum(jnp.where(compact, level_in[:, None, :], 0), axis=2)
    at = slot_of[:, :, None] == jnp.arange(1, rows + 1)[None, None, :]
    compact_own = lax.dynamic_index_in_dim(compact, m, 0, keepdims=False)
    level = lax.dynamic_index_in_dim(level_of, m, 0, keepdims=False)[:, None]
    at_both = jnp.where(m == 0, jnp.concatenate([at[0], at[1]]), jnp.concatenate([at[1], at[0]]))

    send = send.astype(BF)
    land = land.astype(BF)
    at_both = at_both.astype(BF)

    cot = lax.dynamic_slice_in_dim(cotangent, m * half, half, 1)
    buf = pick(land[2], cot, TN).reshape(groups, 2, half)
    x = pick(compact_own, in_x[:, :width])
    part0, part1, buf, x = tie(part0, part1, buf, x)
    near0, near1 = ring_near(part0, "y"), ring_near(part1, "x")
    pieces = ring_rest(near0, "y") + ring_rest(near1, "x")
    back = exchange(buf).reshape(slots, half)
    turn = pick(send[2], land[1])
    buf = pick(turn, back, TN).reshape(groups, 2, half)
    mid = len(pieces) // 2
    late = (mid - 1, 2 * mid - 1)
    crossed = [piece if i in late else swap(piece, "c") for i, piece in enumerate(pieces)]
    *crossed, buf = tie(*crossed, buf)
    for i in late:
        pieces[i], crossed[i] = crossed[i], swap(crossed[i], "c")
    pieces = pieces + crossed
    back = exchange(buf).reshape(slots, half)

    x, xs, nbs, us, g_own, g_other, turned = block_call(
        forward_kernel, "forward", here, pieces, (level, x),
        [
            shape((own, width), BF),
            shape((3, own, width), BF),
            shape((3 * own, width), BF),
            shape((3, own, width), F32),
            shape((3 * own, half), BF),
            shape((3 * own, half), BF),
            shape((width, width), BF),
        ],
        BF,
        dims,
    )
    nbs_far, g_far = swap(nbs, "c"), swap(g_other, "c")
    us, back = tie(us, back)
    both = pick(pick(at_both, send[1], NT), back)
    keep, got = both[:own], swap(both[own:], "m")
    dx = jnp.where(m == 0, jnp.concatenate([keep, got], 1), jnp.concatenate([got, keep], 1))

    x, _ = tie(x, got)
    state = lax.dynamic_slice_in_dim(x, m * half, half, 1)
    state_far = swap(lax.dynamic_slice_in_dim(x, (1 - m) * half, half, 1), "m")

    dx, dybs, du_own, du_other = block_call(
        backward_kernel, "backward", here, pieces + [turned], (level, dx, xs, us),
        [
            shape((own, width), BF),
            shape((3 * own, width), BF),
            shape((3 * own, half), BF),
            shape((3 * own, half), BF),
        ],
        F32,
        dims,
    )
    buf = pick(pick(send[1], at_both, NT), jnp.concatenate([state, state_far], 0)).reshape(groups, 2, half)
    buf = lax.dynamic_update_slice(jnp.zeros((groups, 4, half), BF), buf, (0, 0, 0))
    buf = lax.dynamic_update_slice(buf, pick(compact_own, dx, TN).reshape(groups, 2, half), (0, 2, 0))
    dybs, du_own, du_other, buf = tie(dybs, du_own, du_other, buf)
    dybs_far, du_far = swap(dybs, "c"), swap(du_other, "c")
    moved = exchange(buf)
    back = moved[:, 2:].reshape(groups, width)
    buf = pick(turn, moved[:, :2].reshape(slots, half)).reshape(groups, 2, half)
    moved = exchange(buf).reshape(slots, half)

    sources = [nbs, nbs_far, dybs, dybs_far, du_own, du_far, g_own, g_far]
    used = jnp.any(dev[0][None, :] == jnp.arange(groups)[:, None], axis=1)
    index = jnp.cumsum(used.astype(jnp.int32)) - 1
    pack = (used[None, :] & (index[None, :] == jnp.arange(own)[:, None])).astype(BF)
    grad_keep = pick(pack, back)
    grad_got = swap(grad_keep, "m")
    sum0, sum1 = sum_first(product_call(here, sources, dims), (buf, grad_got))
    sum0, sum1 = sum_second(sum0, sum1)
    keep = pick(land[2], moved)
    sum0, sum1, keep = tie(sum0, sum1, keep)
    total, keep = tie(sum_line(sum0, sum1), keep)
    total, got = sum_ends(total), swap(keep, "m")
    grad_weight = sum_cores(total)
    final = jnp.where(m == 0, jnp.concatenate([keep, got], 1), jnp.concatenate([got, keep], 1))

    by_rank = send[0].reshape(groups, 2, rows)
    place0 = pick(by_rank[:, 0], pack, (((0,), (1,)), ((), ())))
    place1 = pick(by_rank[:, 1], pack, (((0,), (1,)), ((), ())))
    low = jnp.where(m == 0, grad_keep, grad_got)
    high = jnp.where(m == 0, grad_got, grad_keep)
    grad_in = pick(jnp.concatenate([place0, place1], 1), jnp.concatenate([low, high], 0))
    return final, grad_in, grad_weight


def solution(mesh):
    sizes = {128: (4, 4, 4, 2), 16: (2, 2, 2, 2)}[mesh.devices.shape[0]]
    fine = Mesh(mesh.devices.reshape(sizes + (mesh.devices.shape[1],)), DP + ("m",))
    placed = (P(DP, None), P(DP), P(None, DP), P(DP, "m"), P(DP, None))
    return jax.shard_map(
        body,
        mesh=fine,
        in_specs=placed,
        out_specs=(P(DP, None), P(DP, None), P(DP, "m")),
        check_vma=False,
    )
```

```python
import functools

import jax
import jax.numpy as jnp
from jax import lax
from jax.experimental import pallas as pl
from jax.experimental.pallas import tpu as pltpu
from jax.sharding import Mesh, PartitionSpec as P

DP = ("x", "z", "y", "c")
RING = ("m", "z")
BF = jnp.bfloat16
F32 = jnp.float32
NN = (((1,), (0,)), ((), ()))
NT = (((1,), (1,)), ((), ()))
TN = (((0,), (0,)), ((), ()))


def mm(a, b, dims=NN):
    return lax.dot_general(a, b, dims, preferred_element_type=F32)


def pick(sel, rows, dims=NN):
    return mm(sel.astype(BF), rows, dims).astype(BF)


def position(axis):
    if axis == RING:
        return lax.axis_index("m") * lax.axis_size("z") + lax.axis_index("z")
    return lax.axis_index(axis)


def shift(value, axis, k):
    n = lax.axis_size(axis)
    if axis == RING:
        nm, nz = lax.axis_size("m"), lax.axis_size("z")
        order = [(q % nz) * nm + q // nz for q in range(n)]
        return lax.ppermute(value, ("z", "m"), [(order[q], order[(q + k) % n]) for q in range(n)])
    return lax.ppermute(value, axis, [(i, (i + k) % n) for i in range(n)])


def swap(value, axis):
    return shift(value, axis, 1)


def exchange(buf):
    return lax.all_to_all(buf, DP, split_axis=0, concat_axis=0, tiled=True)


def ring_gather(block, axis, dim):
    n = lax.axis_size(axis)
    me = lax.axis_index(axis)
    out = jnp.zeros(block.shape[:dim] + (n,) + block.shape[dim:], block.dtype)
    out = lax.dynamic_update_index_in_dim(out, block, me, dim)
    for k in range(1, n):
        got = shift(block, axis, k)
        out = lax.dynamic_update_index_in_dim(out, got, (me - k + n) % n, dim)
    return out


def ring_scatter(parts, axis, dim):
    n = lax.axis_size(axis)
    me = lax.axis_index(axis)
    total = lax.dynamic_index_in_dim(parts, me, dim, keepdims=False).astype(F32)
    for k in range(1, n):
        piece = lax.dynamic_index_in_dim(parts, (me + k) % n, dim, keepdims=False)
        total = total + shift(piece, axis, k).astype(F32)
    return total


def tie(*values):
    return lax.optimization_barrier(values)


def near_weight(weight):
    half = weight.shape[1] // 2
    c, m = lax.axis_index("c"), lax.axis_index("m")
    mine = lax.dynamic_slice_in_dim(weight, c * half, half, 1)
    other = lax.dynamic_slice_in_dim(weight, (1 - c) * half, half, 1)
    got = swap(other, "c")
    block = jnp.where(c == 0, jnp.concatenate([mine, got], 0), jnp.concatenate([got, mine], 0))
    far = swap(block, "m")
    return jnp.where(m == 0, jnp.stack([block, far]), jnp.stack([far, block]))


def plane_weight(block):
    block = ring_gather(block, "z", 1)
    quarter = block.shape[-1] // 2
    near0, near1 = ring_near(block[..., :quarter], "x"), ring_near(block[..., quarter:], "y")
    return in_order(ring_rest(near0, "x"), "x", 1), in_order(ring_rest(near1, "y"), "y", 2)


def in_order(blocks, axis, dim):
    n = lax.axis_size(axis)
    me = lax.axis_index(axis)
    out = jnp.zeros(blocks[0].shape[:dim] + (n,) + blocks[0].shape[dim:], BF)
    for k, block in zip(distances(n), blocks, strict=True):
        out = lax.dynamic_update_index_in_dim(out, block, (me - k + n) % n, dim)
    return out


def onward(n):
    return [(2 * i + side, 2 * ((i + (n - 1 if side else 1)) % n) + side) for i in range(n) for side in range(2)]


def ring_near(part, axis):
    n = lax.axis_size(axis)
    return [part] + [shift(part, axis, k) for k in distances(n)[1:3]]


def ring_rest(near, axis):
    n = lax.axis_size(axis)
    if n == 2:
        return near
    far = jnp.where(lax.axis_index("c") == 0, near[1], near[2])
    return near + [lax.ppermute(far, (axis, "c"), onward(n))]


def distances(n):
    return [0, 1] if n == 2 else [0, 1, 3, 2]


def load_weight(place, pieces, w_ref, sems):
    nx, ny = w_ref.shape[3], w_ref.shape[5]
    x, y, c = place[0], place[1], place[2]
    kinds = [(0, k) for k in distances(ny)] + [(1, k) for k in distances(nx)]
    copies = {}
    for part, side in enumerate((c, 1 - c)):
        group = pieces[part * len(kinds) : (part + 1) * len(kinds)]
        for ref, (s, k) in zip(group, kinds, strict=True):
            for m in range(2):
                if s == 0:
                    goal = w_ref.at[m, side, 0, :, :, lax.rem(y - k + ny, ny)]
                else:
                    goal = w_ref.at[m, side, 1, lax.rem(x - k + nx, nx)]
                copies[part, s, m, k] = pltpu.make_async_copy(ref.at[m], goal, sems.at[part, s, m, k])
    for copy in copies.values():
        copy.start()
    return copies


def blocks_of(w_ref, place):
    nm, _, ns = w_ref.shape[:3]
    wide = w_ref.shape[-1]
    depth = 1
    for size in w_ref.shape[3:-1]:
        depth *= size
    c = place[2]
    for part, side in enumerate((c, 1 - c)):
        for s in range(ns):
            for m in range(nm):
                first = pl.multiple_of(((m * 2 + side) * ns + s) * wide, wide)
                yield (part, s, m), pl.ds(first, wide), lambda m=m, side=side, s=s: w_ref[m, side, s].reshape(depth, wide)


def arrived(copies, key):
    part, s, m = key
    for name, copy in copies.items():
        if name[:3] == (part, s, m):
            copy.wait()


def norm(x):
    xf = x.astype(F32)
    rinv = lax.rsqrt(jnp.mean(xf * xf, axis=-1, keepdims=True) + 1e-06)
    return xf, rinv


def times_turned(left, wt_ref, parts, store):
    count = wt_ref.shape[1] // parts
    for k in range(parts):
        at = slice(k * count, (k + 1) * count)
        store(at, mm(left, wt_ref[:, at]))


def forward_kernel(n, place, level, x_ref, *refs):
    pieces = refs[:n]
    final, xs, nbs, slopes, g_own, g_other, turned, w_ref, wt_ref, g_ref, y_ref, sems, turn_sem = refs[n:]
    copies = load_weight(place, pieces, w_ref, sems)
    rows, wide = x_ref.shape[0], w_ref.shape[-1]
    x = x_ref[...]
    for step in range(3):
        own = pl.ds(step * rows, rows)
        xf, rinv = norm(x)
        nb = (xf * rinv).astype(BF)
        xs[step] = x
        nbs[own, :] = nb
        for key, cols, block in blocks_of(w_ref, place):
            if step == 0:
                arrived(copies, key)
            part, s, m = key
            w = block()
            if step == 0:
                wt_ref[cols, :] = w.T
            u = mm(nb, w)
            sig = jax.nn.sigmoid(u)
            slopes[step, :, cols] = sig * (1.0 + u * (1.0 - sig))
            g = (u * sig).astype(BF)
            g_ref[:, cols] = g
            out = g_other if part else g_own
            out[own, (s * 2 + m) * wide : (s * 2 + m + 1) * wide] = g
        act = (level[...] >= step + 1).astype(F32)

        def store(at, y, step=step, act=act):
            y_ref[:, at] = (xs[step, :, at].astype(F32) + act * y).astype(BF)

        if step == 0:
            copy = pltpu.make_async_copy(wt_ref, turned, turn_sem)
            copy.start()
        times_turned(g_ref[...], wt_ref, 4, store)
        x = y_ref[...]
    final[...] = x
    copy.wait()


def backward_kernel(n, place, level, dx_ref, *refs):
    pieces, (turned, xs_far, slopes_far) = refs[:n], refs[n : n + 3]
    dx_out, dybs, du_own, du_other, w_ref, wt_ref, du_ref, dn_ref, sems, turn_sem, xs, slopes, in_sems = refs[n + 3 :]
    saved = {}
    for step in (2, 1, 0):
        saved[step] = [
            pltpu.make_async_copy(slopes_far.at[step], slopes.at[step], in_sems.at[0, step]),
            pltpu.make_async_copy(xs_far.at[step], xs.at[step], in_sems.at[1, step]),
        ]
    for copy in saved[2]:
        copy.start()
    copies = load_weight(place, pieces, w_ref, sems)
    for copy in saved[1] + saved[0]:
        copy.start()
    copy = pltpu.make_async_copy(turned, wt_ref, turn_sem)
    copy.start()
    rows, wide = dx_ref.shape[0], w_ref.shape[-1]
    dx_out[...] = dx_ref[...]
    for step in (2, 1, 0):
        own = pl.ds(step * rows, rows)
        act = (level[...] >= step + 1).astype(F32)
        dyb = (act * dx_out[...].astype(F32)).astype(BF)
        dybs[own, :] = dyb
        for saved_copy in saved[step]:
            saved_copy.wait()
        for key, cols, block in blocks_of(w_ref, place):
            if step == 2:
                arrived(copies, key)
            part, s, m = key
            du = (mm(dyb, block()) * slopes[step, :, cols]).astype(BF)
            du_ref[:, cols] = du
            out = du_other if part else du_own
            out[own, (s * 2 + m) * wide : (s * 2 + m + 1) * wide] = du

        def store(at, dn):
            dn_ref[:, at] = dn

        if step == 2:
            copy.wait()
        times_turned(du_ref[...], wt_ref, 4, store)
        xf, rinv = norm(xs[step])
        dn = dn_ref[...]
        mean = jnp.mean(dn * xf, axis=-1, keepdims=True)
        dx = dx_out[...].astype(F32) + rinv * dn - xf * (rinv * rinv * rinv) * mean
        dx_out[...] = dx.astype(BF)


def block_call(kernel, name, place, pieces, operands, outs, last, dims, extra=()):
    nx, nz, ny, rows, wide = dims
    count, width = operands[1].shape
    vmem = pl.BlockSpec(memory_space=pltpu.VMEM)
    work = 36 * count * width * width
    return pl.pallas_call(
        functools.partial(kernel, 4 * (len(distances(nx)) + len(distances(ny))) // 2),
        out_shape=outs,
        in_specs=[pl.BlockSpec(memory_space=pltpu.SMEM)]
        + [vmem] * len(operands)
        + [pl.BlockSpec(memory_space=pl.ANY)] * len(pieces),
        out_specs=[vmem if out.shape != (width, width) else pl.BlockSpec(memory_space=pl.ANY) for out in outs],
        scratch_shapes=[
            pltpu.VMEM((2, 2, 2, nx, nz, ny, rows, wide), BF),
            pltpu.VMEM((width, width), BF),
            pltpu.VMEM((count, width), BF),
            pltpu.VMEM((count, width), last),
            pltpu.SemaphoreType.DMA((2, 2, 2, max(nx, ny))),
            pltpu.SemaphoreType.DMA,
            *extra,
        ],
        compiler_params=pltpu.CompilerParams(vmem_limit_bytes=60 * 2**20),
        cost_estimate=pl.CostEstimate(flops=work, bytes_accessed=12 * 2**20, transcendentals=0),
        name=name,
    )(place, *operands, *pieces)


def product_kernel(place, *refs):
    sources, outs, (left, right, tot0, tot1, sems, out_sems) = refs[:8], refs[8:-6], refs[-6:]
    rows = sources[0].shape[0]
    nx, nz, ny, row, wide = tot0.shape
    copies = []
    for i in range(4):
        copies.append(pltpu.make_async_copy(sources[i], left.at[pl.ds(i * rows, rows)], sems.at[i]))
        copies.append(pltpu.make_async_copy(sources[4 + i], right.at[pl.ds(i * rows, rows)], sems.at[4 + i]))
    for copy in copies:
        copy.start()
    for copy in copies:
        copy.wait()
    chunk = left.shape[1] // nx
    copies = []
    for t in [nx // 2] + [t for t in range(nx) if t != nx // 2]:
        k = lax.rem(place[0] + t, nx)
        cols = left[:, pl.ds(pl.multiple_of(k * chunk, chunk), chunk)]
        full = mm(cols, right[...], TN).astype(BF)
        tot0[t] = full[:, :wide].reshape(nz, ny, row, wide)
        copies.append(pltpu.make_async_copy(tot0.at[t], outs[t], out_sems.at[t]))
        copies[-1].start()
        part = full[:, wide:].reshape(nz, ny, row, wide)
        for y in range(ny):
            tot1[y, k] = part[:, y]
    for t in range(ny):
        copies.append(pltpu.make_async_copy(tot1.at[lax.rem(place[1] + t, ny)], outs[nx + t], out_sems.at[nx + t]))
        copies[-1].start()
    for copy in copies:
        copy.wait()


def product_call(place, sources, dims):
    nx, nz, ny, row, wide = dims
    rows, width = sources[0].shape
    outs = [jax.ShapeDtypeStruct((nz, ny, row, 2 * wide), BF)] * nx
    outs += [jax.ShapeDtypeStruct((nx, nz, row, 2 * wide), BF)] * ny
    outs = pl.pallas_call(
        product_kernel,
        out_shape=outs,
        in_specs=[pl.BlockSpec(memory_space=pltpu.SMEM)] + [pl.BlockSpec(memory_space=pl.ANY)] * 8,
        out_specs=[pl.BlockSpec(memory_space=pl.ANY)] * (nx + ny),
        scratch_shapes=[
            pltpu.VMEM((4 * rows, width), BF),
            pltpu.VMEM((4 * rows, 4 * wide), BF),
            pltpu.VMEM((nx, nz, ny, row, 2 * wide), BF),
            pltpu.VMEM((ny, nx, nz, row, 2 * wide), BF),
            pltpu.SemaphoreType.DMA((8,)),
            pltpu.SemaphoreType.DMA((nx + ny,)),
        ],
        compiler_params=pltpu.CompilerParams(vmem_limit_bytes=60 * 2**20),
        cost_estimate=pl.CostEstimate(flops=96 * rows * width * wide, bytes_accessed=9 * 2**20, transcendentals=0),
        name="products",
    )(place, *sources)
    return outs[:nx], outs[nx:]


def sum_first(groups, after):
    c = lax.axis_index("c")
    near = []
    for axis, pieces in zip(("x", "y"), groups, strict=True):
        if len(pieces) == 4:
            far = lax.ppermute(pieces[2], (axis, "c"), onward(4)).astype(F32)
            up = (pieces[1].astype(F32) + jnp.where(c == 0, far, 0.0)).astype(BF)
            down = (pieces[3].astype(F32) + jnp.where(c == 0, 0.0, far)).astype(BF)
            near.append([pieces[0], shift(up, axis, 1), shift(down, axis, 3)])
        else:
            near.append([pieces[0], shift(pieces[1], axis, 1)])
    near, _ = tie(near, after)
    return [sum((piece.astype(F32) for piece in others), mine.astype(F32)).astype(BF) for mine, *others in near]


def sum_second(sum0, sum1):
    return ring_scatter(sum0, "y", 1).astype(BF), ring_scatter(sum1, "x", 0).astype(BF)


def sum_line(sum0, sum1):
    nz, row, wide = sum0.shape
    tot = jnp.concatenate([sum0.reshape(nz, row, 2, wide // 2), sum1.reshape(nz, row, 2, wide // 2)], axis=-1)
    return ring_scatter(tot, "z", 0).astype(BF)


def sum_ends(tot):
    m = lax.axis_index("m")
    keep = lax.dynamic_index_in_dim(tot, m, 1, keepdims=False)
    send = lax.dynamic_index_in_dim(tot, 1 - m, 1, keepdims=False)
    return keep.astype(F32) + swap(send, "m").astype(F32)


def sum_cores(total):
    c = lax.axis_index("c")
    total = total.reshape(2, -1, total.shape[-1])
    keep = lax.dynamic_index_in_dim(total, c, 0, keepdims=False)
    send = lax.dynamic_index_in_dim(total, 1 - c, 0, keepdims=False)
    got = swap(send, "c")
    return jnp.where(c == 0, jnp.concatenate([keep, got], 1), jnp.concatenate([got, keep], 1))


def body(hidden, depth, destination, weight, cotangent):
    rows, width = hidden.shape
    groups = lax.axis_size(DP)
    slots = 2 * groups
    half = width // 2
    own = rows // 2
    m = lax.axis_index("m")

    dev = destination // rows
    slot = destination % rows
    earlier = jnp.arange(rows)[:, None] > jnp.arange(rows)[None, :]
    rank = jnp.sum((dev[:, :, None] == dev[:, None, :]) & earlier[None], axis=2, dtype=jnp.int32)
    place = dev * 2 + rank
    send = place[:, None, :] == jnp.arange(slots, dtype=jnp.int32)[None, :, None]
    tag = jnp.sum(jnp.where(send, (slot + 1)[:, None, :], 0), axis=2)
    lev = jnp.sum(jnp.where(send[0], depth[None, :], 0), axis=1)
    tags = jnp.concatenate([tag, lev[None]], axis=0).astype(F32)
    tags = tags.reshape(4, groups, 2).transpose(1, 0, 2).reshape(groups, 8).astype(BF)
    tags = jnp.pad(tags, ((0, 0), (0, 120)))
    send_own = lax.dynamic_index_in_dim(send[0].reshape(groups, 2, rows), m, 1, keepdims=False)
    out_x = pick(send_own, hidden)
    buf = jnp.concatenate([out_x, tags], axis=1).reshape(groups, 2, -1)
    block, buf = tie(near_weight(weight), buf)
    in_x = exchange(buf).reshape(groups, -1)
    part0, part1 = plane_weight(block)
    nx, nz, ny = lax.axis_size("x"), lax.axis_size("z"), lax.axis_size("y")
    dims = (nx, nz, ny, 2 * weight.shape[0], weight.shape[1] // 4)
    here = jnp.stack([lax.axis_index("x"), lax.axis_index("y"), lax.axis_index("c")]).astype(jnp.int32)
    shape = jax.ShapeDtypeStruct

    tags = in_x[:, width : width + 8].astype(F32).astype(jnp.int32).reshape(groups, 4, 2)
    tag = tags[:, :3].transpose(1, 0, 2).reshape(3, slots)
    land = tag[:, None, :] == jnp.arange(1, rows + 1, dtype=jnp.int32)[None, :, None]

    first = tags[:, 0].T
    level_in = tags[:, 3].T
    valid = first > 0
    index = jnp.cumsum(valid.astype(jnp.int32), axis=1) - 1
    compact = valid[:, None, :] & (index[:, None, :] == jnp.arange(own)[None, :, None])
    slot_of = jnp.sum(jnp.where(compact, first[:, None, :], 0), axis=2)
    level_of = jnp.sum(jnp.where(compact, level_in[:, None, :], 0), axis=2)
    at = slot_of[:, :, None] == jnp.arange(1, rows + 1)[None, None, :]
    compact_own = lax.dynamic_index_in_dim(compact, m, 0, keepdims=False)
    level = lax.dynamic_index_in_dim(level_of, m, 0, keepdims=False)[:, None]
    at_both = jnp.where(m == 0, jnp.concatenate([at[0], at[1]]), jnp.concatenate([at[1], at[0]]))

    send = send.astype(BF)
    land = land.astype(BF)
    at_both = at_both.astype(BF)

    cot = lax.dynamic_slice_in_dim(cotangent, m * half, half, 1)
    buf = pick(land[2], cot, TN).reshape(groups, 2, half)
    x = pick(compact_own, in_x[:, :width])
    part0, part1, buf, x = tie(part0, part1, buf, x)
    near0, near1 = ring_near(part0, "y"), ring_near(part1, "x")
    pieces = ring_rest(near0, "y") + ring_rest(near1, "x")
    back = exchange(buf).reshape(slots, half)
    turn = pick(send[2], land[1])
    buf = pick(turn, back, TN).reshape(groups, 2, half)
    mid = len(pieces) // 2
    late = (mid - 1, 2 * mid - 1)
    crossed = [piece if i in late else swap(piece, "c") for i, piece in enumerate(pieces)]
    *crossed, buf = tie(*crossed, buf)
    for i in late:
        pieces[i], crossed[i] = crossed[i], swap(crossed[i], "c")
    pieces = pieces + crossed
    back = exchange(buf).reshape(slots, half)

    x, xs, nbs, us, g_own, g_other, turned = block_call(
        forward_kernel, "forward", here, pieces, (level, x),
        [
            shape((own, width), BF),
            shape((3, own, width), BF),
            shape((3 * own, width), BF),
            shape((3, own, width), F32),
            shape((3 * own, half), BF),
            shape((3 * own, half), BF),
            shape((width, width), BF),
        ],
        BF,
        dims,
    )
    nbs_far, g_far = swap(nbs, "c"), swap(g_other, "c")
    us, back = tie(us, back)
    both = pick(pick(at_both, send[1], NT), back)
    keep, got = both[:own], swap(both[own:], "m")
    dx = jnp.where(m == 0, jnp.concatenate([keep, got], 1), jnp.concatenate([got, keep], 1))

    x, _ = tie(x, got)
    state = lax.dynamic_slice_in_dim(x, m * half, half, 1)
    state_far = swap(lax.dynamic_slice_in_dim(x, (1 - m) * half, half, 1), "m")

    dx, dybs, du_own, du_other = block_call(
        backward_kernel, "backward", here, pieces + [turned, xs, us], (level, dx),
        [
            shape((own, width), BF),
            shape((3 * own, width), BF),
            shape((3 * own, half), BF),
            shape((3 * own, half), BF),
        ],
        F32,
        dims,
        [pltpu.VMEM(xs.shape, BF), pltpu.VMEM(us.shape, F32), pltpu.SemaphoreType.DMA((2, 3))],
    )
    buf = pick(pick(send[1], at_both, NT), jnp.concatenate([state, state_far], 0)).reshape(groups, 2, half)
    buf = lax.dynamic_update_slice(jnp.zeros((groups, 4, half), BF), buf, (0, 0, 0))
    buf = lax.dynamic_update_slice(buf, pick(compact_own, dx, TN).reshape(groups, 2, half), (0, 2, 0))
    dybs, du_own, du_other, buf = tie(dybs, du_own, du_other, buf)
    dybs_far, du_far = swap(dybs, "c"), swap(du_other, "c")
    moved = exchange(buf)
    back = moved[:, 2:].reshape(groups, width)
    buf = pick(turn, moved[:, :2].reshape(slots, half)).reshape(groups, 2, half)
    moved = exchange(buf).reshape(slots, half)

    sources = [nbs, nbs_far, dybs, dybs_far, du_own, du_far, g_own, g_far]
    used = jnp.any(dev[0][None, :] == jnp.arange(groups)[:, None], axis=1)
    index = jnp.cumsum(used.astype(jnp.int32)) - 1
    pack = (used[None, :] & (index[None, :] == jnp.arange(own)[:, None])).astype(BF)
    grad_keep = pick(pack, back)
    grad_got = swap(grad_keep, "m")
    sum0, sum1 = sum_first(product_call(here, sources, dims), (buf, grad_got))
    sum0, sum1 = sum_second(sum0, sum1)
    keep = pick(land[2], moved)
    sum0, sum1, keep = tie(sum0, sum1, keep)
    total, keep = tie(sum_line(sum0, sum1), keep)
    total, got = sum_ends(total), swap(keep, "m")
    grad_weight = sum_cores(total)
    final = jnp.where(m == 0, jnp.concatenate([keep, got], 1), jnp.concatenate([got, keep], 1))

    by_rank = send[0].reshape(groups, 2, rows)
    place0 = pick(by_rank[:, 0], pack, (((0,), (1,)), ((), ())))
    place1 = pick(by_rank[:, 1], pack, (((0,), (1,)), ((), ())))
    low = jnp.where(m == 0, grad_keep, grad_got)
    high = jnp.where(m == 0, grad_got, grad_keep)
    grad_in = pick(jnp.concatenate([place0, place1], 1), jnp.concatenate([low, high], 0))
    return final, grad_in, grad_weight


def solution(mesh):
    sizes = {128: (4, 4, 4, 2), 16: (2, 2, 2, 2)}[mesh.devices.shape[0]]
    fine = Mesh(mesh.devices.reshape(sizes + (mesh.devices.shape[1],)), DP + ("m",))
    placed = (P(DP, None), P(DP), P(None, DP), P(DP, "m"), P(DP, None))
    return jax.shard_map(
        body,
        mesh=fine,
        in_specs=placed,
        out_specs=(P(DP, None), P(DP, None), P(DP, "m")),
        check_vma=False,
    )
```
